256 devices in a mesh: tm: 8 (over y_hi, x), height: 32 (over y_lo, z, core).
Axes of the slice: x: 4, y: 4 (y_hi: 2, y_lo: 2; y = y_hi * 2 + y_lo), z: 8, core: 2. Of those that a mesh axis runs over, the one named last changes fastest.
Arguments:
- queries: bfloat16 [16, 256, 32, 1280], P('tm', 'height'), may hold values from -6.4 to 6.4
- keys: bfloat16 [16, 256, 32, 1280], P('tm', 'height'), may hold values from -6.4 to 6.4
- values: bfloat16 [16, 256, 32, 1280], P('tm', 'height'), may hold values from -6 to 6
- widths: int32 [16], replicated, may hold values from 16 to 32, as said below
Outputs:
- attended: bfloat16 [16, 256, 32, 1280], P('tm', 'height')
The draws below stay inside these ranges and needn't reach their ends.
Inputs may be any that keep to these rules, and one draw needn't show every extreme that they name: `widths`: every frame has 16 to 32 valid columns; at least one frame has 32 and at least one has 16.
All inputs are finite; a program needn't handle non-finite values.
Results may differ from the reference program's by a relative error of at most 0.0049.
Values may be sent and summed in bfloat16 or wider, within the bound.
A program may use at most 64 MiB of HBM per device.

```python
import math
import jax
import jax.numpy as jnp
from jax import lax

HEADS = 10
HD = 128
TSPAN = 1
RSPAN = 4
COLS = 32
HW = 1280
NT = 16
NH = 256


def draw_queries(key, part):
    key = jax.random.fold_in(key, 1)
    field = jax.random.truncated_normal(key, -4.5, 4.5, (NT, NH, COLS, HEADS, HD)) * 1.4
    return field.reshape(NT, NH, COLS, HEADS * HD).astype(jnp.float32).astype(jnp.bfloat16)


def draw_keys(key, part):
    key = jax.random.fold_in(key, 2)
    field = jax.random.truncated_normal(key, -4.5, 4.5, (NT, NH, COLS, HEADS, HD)) * 1.4
    return field.reshape(NT, NH, COLS, HEADS * HD).astype(jnp.float32).astype(jnp.bfloat16)


def draw_widths(key, part):
    key = jax.random.fold_in(key, 3)
    counts = jax.random.randint(jax.random.fold_in(key, 1), (NT,), COLS // 2, COLS + 1)
    first = jax.random.randint(jax.random.fold_in(key, 2), (), 0, NT)
    second = (first + 1 + jax.random.randint(jax.random.fold_in(key, 4), (), 0, NT - 1)) % NT
    counts = counts.at[first].set(COLS)
    counts = counts.at[second].set(COLS // 2)
    return counts.astype(jnp.int32)


def level_of(rng, extent, cuts, low, largest):
    factor_of = 1.0
    for axis_at, blocks in cuts:
        heights = jax.random.uniform(jax.random.fold_in(jax.random.fold_in(rng, 6), axis_at), (blocks,), jnp.float32, low / len(cuts), largest / len(cuts))
        factor_of = factor_of * jnp.repeat(jnp.exp(heights), extent[axis_at] // blocks).reshape((-1,) + (1,) * (len(extent) - 1 - axis_at))
    return factor_of


def gaussian(stream_key, dims, deviation, bound, cuts=(), held_as=jnp.bfloat16):
    array = deviation * jax.random.normal(stream_key, dims, jnp.float32)
    if cuts:
        array = array * level_of(stream_key, dims, cuts, -0.22, 0.18)
    return jnp.clip(array, -bound, bound).astype(held_as)


def setup_inputs(seed: int = 0) -> dict:
    splits = jax.random.split(jax.random.key(seed), 5)
    queries = draw_queries(jax.random.fold_in(splits[4], 71), 0)
    keys = draw_keys(jax.random.fold_in(splits[4], 71), 0)
    values = gaussian(splits[2], (NT, NH, COLS, HW), 1.0, 6.0, ((0, 8), (1, 32)))
    widths = draw_widths(jax.random.fold_in(splits[4], 71), 0)
    return dict(queries=queries, keys=keys, values=values, widths=widths)


def key_mask(frame_ids, row_ids, widths, col_count, row_total):
    table = jnp.arange(widths.shape[0], dtype=jnp.int32)
    frame_width = lax.optimization_barrier(jnp.sum(jnp.where(frame_ids[:, None] == table[None, :], widths[None, :], 0), axis=1))
    row_inside = (row_ids >= 0) & (row_ids < row_total)
    columns = jnp.arange(col_count, dtype=jnp.int32)
    inside = (columns[None, None, :] < frame_width[:, None, None]) & row_inside[None, :, None]
    return inside.reshape(-1)

def attend(query_rows, key_rows, value_rows, allowed):
    head_count = query_rows.shape[2] // HD

    def split_heads(block):
        return block.reshape(block.shape[0], block.shape[1], head_count, HD).transpose(2, 0, 1, 3)

    def one_head(head_parts):
        head_q, head_k, head_v = head_parts
        scores = jnp.einsum('bnd,bmd->bnm', head_q.astype(jnp.float32), head_k.astype(jnp.float32)) / math.sqrt(HD)
        scores = jnp.where(allowed, scores, -jnp.inf)
        top_score = lax.optimization_barrier(jnp.max(scores, axis=2, keepdims=True))
        exp_scores = jnp.exp(scores - top_score)
        weights = (exp_scores / lax.optimization_barrier(jnp.sum(exp_scores, axis=2, keepdims=True))).astype(jnp.bfloat16)
        return jnp.einsum('bnm,bmd->bnd', weights.astype(jnp.float32), head_v.astype(jnp.float32))
    mixed = lax.map(one_head, (split_heads(query_rows), split_heads(key_rows), split_heads(value_rows)))
    return mixed.transpose(1, 2, 0, 3).reshape(query_rows.shape).astype(jnp.bfloat16)

def reference(queries, keys, values, widths):
    frame_span = TSPAN
    row_span = RSPAN
    time_wide = 2 * frame_span
    row_wide = 2 * row_span
    frame_total, row_total, col_count, feat_width = queries.shape
    margins = ((frame_span, frame_span), (row_span, row_span), (0, 0), (0, 0))
    padded = [jnp.pad(field, margins) for field in (queries, keys, values)]
    time_bins = frame_total // time_wide + 1
    row_bins = row_total // row_wide + 1
    token_count = time_wide * row_wide * col_count

    def window(index):
        time_bin = index // row_bins
        row_bin = index % row_bins
        start = (time_bin * time_wide, row_bin * row_wide, jnp.int32(0), jnp.int32(0))
        pieces = [lax.dynamic_slice(field, start, (time_wide, row_wide, col_count, feat_width)).reshape(1, token_count, feat_width) for field in padded]
        frame_ids = (time_bin * time_wide - frame_span + jnp.arange(time_wide, dtype=jnp.int32)).astype(jnp.int32)
        row_ids = (row_bin * row_wide - row_span + jnp.arange(row_wide, dtype=jnp.int32)).astype(jnp.int32)
        inside = key_mask(frame_ids, row_ids, widths, col_count, row_total)
        allowed = inside[None, :] | jnp.eye(token_count, dtype=jnp.bool_)
        result = attend(pieces[0], pieces[1], pieces[2], allowed[None])
        return result[0].reshape(time_wide, row_wide, col_count, feat_width)
    stacked = lax.map(window, jnp.arange(time_bins * row_bins, dtype=jnp.int32))
    stacked = stacked.reshape(time_bins, row_bins, time_wide, row_wide, col_count, feat_width)
    stacked = stacked.transpose(0, 2, 1, 3, 4, 5).reshape(time_bins * time_wide, row_bins * row_wide, col_count, feat_width)
    return stacked[frame_span:frame_span + frame_total, row_span:row_span + row_total]
```

```python
import math

import jax
import jax.numpy as jnp
from jax import lax
from jax.experimental import pallas as pl
from jax.experimental.pallas import tpu as pltpu
from jax.sharding import PartitionSpec as P

HD = 128
MESH = pl.DeviceIdType.MESH
AHEAD = 2


def on_device(queries, keys, values, widths):
    frames, rows, cols, feats = queries.shape
    heads = feats // HD
    span_f, span_r = frames // 2, rows // 2
    tm_count, height_count = lax.axis_size("tm"), lax.axis_size("height")
    quarter = span_f * span_r * cols
    window = 4 * quarter
    factor = math.log2(math.e) / math.sqrt(HD)

    def kernel(
        w_ref, q_ref, k_ref, v_ref, o_ref, qs, kv, os, bias, local_sem, out_sem, send_sem, recv_sem
    ):
        t, h = lax.axis_index("tm"), lax.axis_index("height")
        places = ((t + 1, h), (t - 1, h), (t, h + 1), (t, h - 1))
        there = (t < tm_count - 1, t > 0, h < height_count - 1, h > 0)

        def local(g):
            lanes = pl.ds(pl.multiple_of(g * HD, HD), HD)
            own = (pl.ds(span_f, frames), pl.ds(span_r, rows))
            return (
                pltpu.make_async_copy(
                    k_ref.at[:, :, :, lanes], kv.at[g, 0, own[0], own[1]], local_sem.at[0, g]
                ),
                pltpu.make_async_copy(
                    v_ref.at[:, :, :, lanes], kv.at[g, 1, own[0], own[1]], local_sem.at[1, g]
                ),
                pltpu.make_async_copy(q_ref.at[:, :, :, lanes], qs.at[g], local_sem.at[2, g]),
            )

        def result(g):
            lanes = pl.ds(pl.multiple_of(g * HD, HD), HD)
            return pltpu.make_async_copy(os.at[g], o_ref.at[:, :, :, lanes], out_sem.at[g])

        own_rows = (span_r, rows)
        moves = (
            (0, None, (2, 1), own_rows, (0, 1), own_rows),
            (1, None, (1, 1), own_rows, (3, 1), own_rows),
            (2, None, (1, 2), (8, 4), (1, 2), (0, 4)),
            (3, None, (1, 2), (4, 4), (1, 2), (12, 4)),
            (2, 1, (0, 1), (8, 4), (0, 1), (0, 4)),
            (3, 1, (0, 1), (4, 4), (0, 1), (12, 4)),
            (2, 0, (3, 1), (8, 4), (3, 1), (0, 4)),
            (3, 0, (3, 1), (4, 4), (3, 1), (12, 4)),
        )
        opposite = (1, 0, 3, 2)

        def move(m, g):
            to, _, sf, sr, df, dr = moves[m]
            return pltpu.make_async_remote_copy(
                src_ref=kv.at[g, :, pl.ds(*sf), pl.ds(*sr)],
                dst_ref=kv.at[g, :, pl.ds(*df), pl.ds(*dr)],
                send_sem=send_sem.at[m, g],
                recv_sem=recv_sem.at[m, g],
                device_id=places[to],
                device_id_type=MESH,
            )

        def sends(m):
            to, via = moves[m][:2]
            return there[to] if via is None else there[to] & there[via]

        def receives(m):
            to, via = moves[m][:2]
            return there[opposite[to]] if via is None else there[opposite[to]] & there[via]

        def start(m, g):
            @pl.when(sends(m))
            def _():
                move(m, g).start()

        def arrive(m, g):
            @pl.when(receives(m))
            def _():
                move(m, g).wait_recv()

        @pl.loop(0, heads)
        def _(g):
            for copy in local(g):
                copy.start()

        barrier = pltpu.get_barrier_semaphore()
        for place, present in zip(places, there):

            @pl.when(present)
            def _():
                pl.semaphore_signal(barrier, inc=1, device_id=place, device_id_type=MESH)

        for present, where in (
            (there[1], (pl.ds(0, 1), slice(None))),
            (there[0], (pl.ds(3, 1), slice(None))),
            (there[3], (slice(None), pl.ds(0, 4))),
            (there[2], (slice(None), pl.ds(12, 4))),
        ):

            @pl.when(jnp.logical_not(present))
            def _():
                @pl.loop(0, heads)
                def _(g):
                    for part in range(2):
                        block = kv.at[g, part, where[0], where[1]]
                        block[...] = jnp.zeros(block.shape, block.dtype)

        key = lax.broadcasted_iota(jnp.int32, (quarter, window), 1)
        query = lax.broadcasted_iota(jnp.int32, (quarter, window), 0)
        half = window // 2
        for a in range(2):
            for b in range(2):
                first = t * frames - span_f + 2 * a
                size = []
                for frame in (first, first + 1):
                    inside = (frame >= 0) & (frame < tm_count * frames)
                    width = w_ref[jnp.clip(frame, 0, tm_count * frames - 1)]
                    size.append(jnp.where(inside, width, 0))
                row = (key // cols) % rows + (h * rows - span_r + rows * b)
                width = jnp.where(key < half, size[0], size[1])
                ok = (key % cols < width) & (row >= 0) & (row < height_count * rows)
                same = key == query + ((1 - a) * half + (4 - 4 * b) * cols)
                bias[a, b] = jnp.where(ok | same, 0.0, -1e30).astype(jnp.float32)

        total = jnp.int32(0)
        for present in there:
            total = total + present.astype(jnp.int32)
        pl.semaphore_wait(barrier, total)

        @pl.loop(0, heads)
        def _(g):
            copies = local(g)
            copies[0].wait()
            copies[1].wait()
            start(0, g)
            start(1, g)

            @pl.when(g < AHEAD)
            def _():
                start(2, g)
                start(3, g)

        def relay(g):
            arrive(0, g)
            start(4, g)
            start(5, g)
            arrive(1, g)
            start(6, g)
            start(7, g)

        def compute(g):
            for m in range(2, 8):
                arrive(m, g)
            local(g)[2].wait()
            for a in range(2):
                for b in range(2):
                    q = qs[g, a, pl.ds(4 * b, 4)].reshape(quarter, HD)
                    k = kv[g, 0, pl.ds(2 * a, 2), pl.ds(8 * b, 8)].reshape(window, HD)
                    v = kv[g, 1, pl.ds(2 * a, 2), pl.ds(8 * b, 8)].reshape(window, HD)
                    s = lax.dot_general(
                        q, k, (((1,), (1,)), ((), ())), preferred_element_type=jnp.float32
                    )
                    s = s + bias[a, b]
                    top = jnp.max(s, axis=1, keepdims=True)
                    p = jnp.exp2((s - top) * factor)
                    p = p * (1.0 / jnp.sum(p, axis=1, keepdims=True))
                    out = jnp.dot(p.astype(jnp.bfloat16), v, preferred_element_type=jnp.float32)
                    os[g, a, pl.ds(4 * b, 4)] = out.astype(jnp.bfloat16).reshape(
                        span_r, cols, HD
                    )
            result(g).start()

        @pl.loop(0, heads + 1)
        def _(g):
            @pl.when(g < heads)
            def _():
                relay(g)

            @pl.when(g + AHEAD < heads)
            def _():
                start(2, g + AHEAD)
                start(3, g + AHEAD)

            @pl.when(g > 0)
            def _():
                compute(g - 1)

        @pl.loop(0, heads)
        def _(g):
            for m in range(8):

                @pl.when(sends(m))
                def _():
                    move(m, g).wait_send()

            result(g).wait()

    any_space = pl.BlockSpec(memory_space=pl.ANY)
    return pl.pallas_call(
        kernel,
        out_shape=jax.ShapeDtypeStruct(queries.shape, queries.dtype),
        in_specs=[pl.BlockSpec(memory_space=pltpu.SMEM)] + [any_space] * 3,
        out_specs=any_space,
        scratch_shapes=[
            pltpu.VMEM((heads, frames, rows, cols, HD), jnp.bfloat16),
            pltpu.VMEM((heads, 2, 2 * frames, 2 * rows, cols, HD), jnp.bfloat16),
            pltpu.VMEM((heads, frames, rows, cols, HD), jnp.bfloat16),
            pltpu.VMEM((2, 2, quarter, window), jnp.float32),
            pltpu.SemaphoreType.DMA((3, heads)),
            pltpu.SemaphoreType.DMA((heads,)),
            pltpu.SemaphoreType.DMA((8, heads)),
            pltpu.SemaphoreType.DMA((8, heads)),
        ],
        compiler_params=pltpu.CompilerParams(
            collective_id=0, has_side_effects=True, vmem_limit_bytes=40 * 2**20
        ),
    )(widths, queries, keys, values)


def solution(mesh):
    placed = P("tm", "height", None, None)
    return jax.shard_map(
        on_device,
        mesh=mesh,
        in_specs=(placed, placed, placed, P()),
        out_specs=placed,
        check_vma=False,
    )
```

```python
import math

import jax
import jax.numpy as jnp
from jax import lax
from jax.experimental import pallas as pl
from jax.experimental.pallas import tpu as pltpu
from jax.sharding import PartitionSpec as P

HD = 128
MESH = pl.DeviceIdType.MESH
X_AHEAD = 10
Q_AHEAD = 10
LAG = 2
BYPASS = 2
VMEM = 62 * 2**20


def on_device(queries, keys, values, widths):
    frames, rows, cols, feats = queries.shape
    heads = feats // HD
    half = rows // 2
    tm_count, height_count = lax.axis_size("tm"), lax.axis_size("height")
    frame_total = tm_count * frames
    quarter = half * cols
    pair = 2 * quarter
    factor = math.log2(math.e) / math.sqrt(HD)

    def kernel(
        w_hbm,
        q_ref,
        k_ref,
        v_ref,
        o_ref,
        w_ref,
        qs,
        qn,
        kv,
        sib,
        hold,
        part_o,
        part_l,
        send_o,
        send_l,
        got_o,
        got_l,
        os,
        bias,
        w_sem,
        local_sem,
        out_sem,
        send_sem,
        x_sem,
        q_sem,
        o_sem,
        l_sem,
        own_sem,
        fwd_sem,
        hold_sem,
    ):
        t, h = lax.axis_index("tm"), lax.axis_index("height")
        core = lax.rem(h, 2)
        far = h - 1 + 2 * core
        near = h + 1 - 2 * core
        has_far = (far >= 0) & (far < height_count)
        first_row = (half * core, half * (1 - core))
        has_next, has_prev = t < tm_count - 1, t > 0
        mid = tm_count // 2
        ends = (0, tm_count - 1)
        is_mid = (t == mid - 1) | (t == mid)
        is_end = (t == 0) | (t == tm_count - 1)

        def lanes(g):
            return pl.ds(pl.multiple_of(g * HD, HD), HD)

        def local_kv(side, g):
            at = pl.ds(first_row[side], half)
            return tuple(
                pltpu.make_async_copy(
                    ref.at[:, at, :, lanes(g)],
                    kv.at[g, side, part, pl.ds(1, frames)],
                    local_sem.at[side, part, g],
                )
                for part, ref in enumerate((k_ref, v_ref))
            )

        def local_q(side, g):
            at = pl.ds(first_row[side], half)
            return pltpu.make_async_copy(
                q_ref.at[:, at, :, lanes(g)], qs.at[g, side], local_sem.at[side, 2, g]
            )

        def result(g):
            return pltpu.make_async_copy(os.at[g], o_ref.at[:, :, :, lanes(g)], out_sem)

        def remote(src, dst, send, recv, to):
            return pltpu.make_async_remote_copy(
                src_ref=src,
                dst_ref=dst,
                send_sem=send_sem.at[send],
                recv_sem=recv,
                device_id=to,
                device_id_type=MESH,
            )

        x_from, x_into = (2, 1), (0, 3)
        step_to = ((t + 1, h), (t - 1, h))
        x_sends, x_gets = (has_next, has_prev), (has_prev, has_next)
        detours = ((mid - 1, ends[1], mid), (mid, ends[0], mid - 1))
        turn = height_count // 2
        outer = (h < 2) | (h >= height_count - 2)
        inner_rows = (h >= turn - 2) & (h < turn + 2)
        other = lax.rem(h + turn, height_count)

        def x_copy(way, side, g):
            return remote(
                kv.at[g, side, :, pl.ds(x_from[way], 1)],
                kv.at[g, side, :, pl.ds(x_into[way], 1)],
                way,
                x_sem.at[way, side, g],
                step_to[way],
            )

        def first_leg(way, side, g, row):
            return remote(
                kv.at[g, side, :, pl.ds(x_from[way], 1)],
                hold.at[side, g],
                way,
                hold_sem.at[side, g],
                (detours[way][1], row),
            )

        def second_leg(way, side, g, row):
            return remote(
                hold.at[side, g],
                kv.at[g, side, :, pl.ds(x_into[way], 1)],
                (2, 9)[side],
                x_sem.at[way, side, g],
                (detours[way][2], row),
            )

        def goes_round(side, g):
            turns = lax.rem(g, BYPASS) == 0
            if side == 0:
                turns = turns & jnp.logical_not(outer | inner_rows)
            return turns

        def begin_x(side, g):
            for copy in local_kv(side, g):
                copy.wait()
            for way in range(2):
                round_trip = (t == detours[way][0]) & goes_round(side, g)

                @pl.when(round_trip)
                def _():
                    first_leg(way, side, g, h).start()

                direct = x_sends[way] & jnp.logical_not(round_trip)
                if side == 0:
                    far_trip = (t == detours[way][0]) & outer

                    @pl.when(far_trip)
                    def _():
                        first_leg(way, side, g, other).start()

                    direct = direct & jnp.logical_not(far_trip)

                @pl.when(direct)
                def _():
                    x_copy(way, side, g).start()

        def begin_step(step):
            @pl.when(step < heads)
            def _():
                begin_x(0, step)

            @pl.when((step >= heads) & (step < 2 * heads))
            def _():
                begin_x(1, step - heads)

        def arrive_x(way, side, g):
            @pl.when(x_gets[way])
            def _():
                x_copy(way, side, g).wait_recv()

        def pass_on(side, g):
            for way in range(2):

                @pl.when((t == detours[way][1]) & goes_round(side, g))
                def _():
                    first_leg(way, side, g, h).wait_recv()
                    second_leg(way, side, g, h).start()

                if side == 0:

                    @pl.when((t == detours[way][1]) & inner_rows)
                    def _():
                        first_leg(way, side, g, other).wait_recv()
                        second_leg(way, side, g, other).start()

        def q_copy(g):
            return remote(qs.at[g, 0], qn.at[g], 3, q_sem.at[g], (t, far))

        def o_copy(g):
            return remote(send_o.at[g], got_o.at[g], 4, o_sem.at[g], (t, far))

        def l_copy(g):
            return remote(send_l.at[g], got_l.at[g], 5, l_sem.at[g], (t, far))

        def own_copy(g):
            return remote(
                kv.at[g, 1, :, pl.ds(1, frames)],
                sib.at[g, :, pl.ds(1, frames)],
                6,
                own_sem.at[g],
                (t, near),
            )

        def fwd_copy(way, g):
            return remote(
                kv.at[g, 1, :, pl.ds(x_into[way], 1)],
                sib.at[g, :, pl.ds(x_into[way], 1)],
                7 + way,
                fwd_sem.at[way, g],
                (t, near),
            )

        def begin_q(g):
            local_q(0, g).wait()

            @pl.when(has_far)
            def _():
                q_copy(g).start()

        @pl.loop(0, heads)
        def _(g):
            for copy in local_kv(0, g):
                copy.start()

        barrier = pltpu.get_barrier_semaphore()
        greeted = [(has_next, (t + 1, h)), (has_prev, (t - 1, h)), (has_far, (t, far))]
        greeted += [(is_mid, (at, h)) for at in ends]
        greeted += [(is_end, (at, h)) for at in (mid - 1, mid)]
        greeted += [(is_mid & outer, (at, other)) for at in ends]
        greeted += [(is_end & inner_rows, (at, other)) for at in (mid - 1, mid)]
        total = jnp.int32(1)
        pl.semaphore_signal(barrier, inc=1, device_id=(t, near), device_id_type=MESH)
        for present, place in greeted:
            total = total + present.astype(jnp.int32)

            @pl.when(present)
            def _():
                pl.semaphore_signal(barrier, inc=1, device_id=place, device_id_type=MESH)

        sizes = pltpu.make_async_copy(w_hbm, w_ref, w_sem)
        sizes.start()

        @pl.loop(0, heads)
        def _(g):
            local_q(0, g).start()

        pl.semaphore_wait(barrier, total)

        @pl.loop(0, min(X_AHEAD, heads))
        def _(g):
            begin_x(0, g)

            @pl.when(g < Q_AHEAD)
            def _():
                begin_q(g)

        @pl.loop(0, heads)
        def _(g):
            for copy in local_kv(1, g):
                copy.start()
            local_q(1, g).start()

        @pl.loop(heads, max(X_AHEAD, heads))
        def _(g):
            begin_step(g)

        for present, at in ((has_prev, 0), (has_next, 3)):

            @pl.when(jnp.logical_not(present))
            def _():
                @pl.loop(0, heads)
                def _(g):
                    for part in range(2):
                        for block in (kv.at[g, 0, part, at], kv.at[g, 1, part, at]):
                            block[...] = jnp.zeros(block.shape, block.dtype)
                        sib[g, part, at] = jnp.zeros((half, cols, HD), sib.dtype)

        @pl.when(jnp.logical_not(has_far))
        def _():
            @pl.loop(0, heads)
            def _(g):
                qn[g] = jnp.zeros(qn.shape[1:], qn.dtype)
                got_o[g] = jnp.zeros(got_o.shape[1:], got_o.dtype)
                got_l[g] = jnp.full(got_l.shape[1:], -1e30, got_l.dtype)

        sizes.wait()
        key = lax.broadcasted_iota(jnp.int32, (pair, pair), 1)
        query = lax.broadcasted_iota(jnp.int32, (pair, pair), 0)
        for a in range(2):
            size = []
            for frame in (t * frames - 1 + 2 * a, t * frames + 2 * a):
                inside = (frame >= 0) & (frame < frame_total)
                width = w_ref[jnp.clip(frame, 0, frame_total - 1)]
                size.append(jnp.where(inside, width, 0))
            width = jnp.where(key < quarter, size[0], size[1])
            same = (query < quarter) & (key == query + (1 - a) * quarter)
            ok = (key % cols < width) | same
            bias[a] = jnp.where(ok, 0.0, -1e30).astype(jnp.float32)

        eye = lax.broadcasted_iota(jnp.int32, (quarter, quarter), 0) == (
            lax.broadcasted_iota(jnp.int32, (quarter, quarter), 1)
        )

        def to_row(column):
            return jnp.sum(jnp.where(eye, column, 0.0), axis=0, keepdims=True)

        def to_column(row):
            return jnp.sum(jnp.where(eye, row, 0.0), axis=1, keepdims=True)

        def inner(x, y):
            return lax.dot_general(
                x, y, (((1,), (1,)), ((), ())), preferred_element_type=jnp.float32
            )

        first = lax.broadcasted_iota(jnp.int32, (8, quarter), 0) == 0

        def shares(g):
            logs = []
            for a in range(2):
                q = jnp.concatenate(
                    [qs[g, 0, a].reshape(quarter, HD), qn[g, a].reshape(quarter, HD)], axis=0
                )
                k = kv[g, 0, 0, pl.ds(2 * a, 2)].reshape(pair, HD)
                v = kv[g, 0, 1, pl.ds(2 * a, 2)].reshape(pair, HD)
                s = inner(q, k) + bias[a]
                top = jnp.max(s, axis=1, keepdims=True)
                p = jnp.exp2((s - top) * factor)
                total = jnp.sum(p, axis=1, keepdims=True)
                out = jnp.dot(p.astype(jnp.bfloat16), v, preferred_element_type=jnp.float32)
                out = out * (1.0 / total)
                logs.append(top * factor + jnp.log2(total))
                part_o[g, a] = out[:quarter]
                send_o[g, a] = out[quarter:].astype(jnp.bfloat16).reshape(half, cols, HD)
            part_l[g] = jnp.where(first, to_row(logs[0][:quarter]), to_row(logs[1][:quarter]))
            send_l[g] = jnp.where(first, to_row(logs[0][quarter:]), to_row(logs[1][quarter:]))

        def merge(g):
            @pl.when(has_far)
            def _():
                o_copy(g).wait_recv()
                l_copy(g).wait_recv()

            weight = 1.0 / (1.0 + jnp.exp2(got_l[g] - part_l[g]))
            for a in range(2):
                mine = to_column(weight[a : a + 1])
                other = got_o[g, a].reshape(quarter, HD).astype(jnp.float32)
                out = other + mine * (part_o[g, a] - other)
                os[g, a, pl.ds(first_row[0], half)] = out.astype(jnp.bfloat16).reshape(
                    half, cols, HD
                )

        def whole(g):
            local_q(1, g).wait()
            own_copy(g).wait_recv()
            for way in range(2):

                @pl.when(x_gets[way])
                def _():
                    fwd_copy(way, g).wait_recv()

            for a in range(2):
                q = qs[g, 1, a].reshape(quarter, HD)
                at = pl.ds(2 * a, 2)
                s1 = inner(q, kv[g, 1, 0, at].reshape(pair, HD)) + bias[a, pl.ds(0, quarter)]
                s2 = inner(q, sib[g, 0, at].reshape(pair, HD)) + bias[a, pl.ds(quarter, quarter)]
                top = jnp.maximum(
                    jnp.max(s1, axis=1, keepdims=True), jnp.max(s2, axis=1, keepdims=True)
                )
                p1 = jnp.exp2((s1 - top) * factor)
                p2 = jnp.exp2((s2 - top) * factor)
                total = jnp.sum(p1, axis=1, keepdims=True) + jnp.sum(p2, axis=1, keepdims=True)
                v1 = kv[g, 1, 1, at].reshape(pair, HD)
                v2 = sib[g, 1, at].reshape(pair, HD)
                out = jnp.dot(p1.astype(jnp.bfloat16), v1, preferred_element_type=jnp.float32)
                out += jnp.dot(p2.astype(jnp.bfloat16), v2, preferred_element_type=jnp.float32)
                out = out * (1.0 / total)
                os[g, a, pl.ds(first_row[1], half)] = out.astype(jnp.bfloat16).reshape(
                    half, cols, HD
                )

        @pl.loop(0, heads)
        def _(g):
            pass_on(0, g)
            arrive_x(0, 0, g)
            arrive_x(1, 0, g)
            begin_step(g + X_AHEAD)

            @pl.when(g + Q_AHEAD < heads)
            def _():
                begin_q(g + Q_AHEAD)

            @pl.when(has_far)
            def _():
                q_copy(g).wait_recv()

            shares(g)

            @pl.when(has_far)
            def _():
                o_copy(g).start()
                l_copy(g).start()

        @pl.loop(0, heads + LAG)
        def _(g):
            @pl.when(g >= LAG)
            def _():
                merge(g - LAG)
                whole(g - LAG)
                result(g - LAG).start()

            @pl.when(g < heads)
            def _():
                own_copy(g).start()
                pass_on(1, g)
                for way in range(2):
                    arrive_x(way, 1, g)

                    @pl.when(x_gets[way])
                    def _():
                        fwd_copy(way, g).start()

                begin_step(heads + g + X_AHEAD)

        def sent(index, ref):
            remote(ref, ref, index, hold_sem.at[0, 0], (t, near)).wait_send()

        for way in range(2):

            @pl.when(x_sends[way])
            def _():
                sent(way, kv.at[:, :, :, pl.ds(x_from[way], 1)])

            @pl.when(x_gets[way])
            def _():
                sent(7 + way, kv.at[:, 1, :, pl.ds(x_into[way], 1)])

        some = pl.ds(0, (heads + BYPASS - 1) // BYPASS)

        @pl.when(is_end & inner_rows)
        def _():
            sent(2, hold.at[0])

        @pl.when(is_end & jnp.logical_not(outer | inner_rows))
        def _():
            sent(2, hold.at[0, some])

        @pl.when(is_end)
        def _():
            sent(9, hold.at[1, some])

        @pl.when(has_far)
        def _():
            sent(3, qn)
            sent(4, send_o)
            sent(5, send_l)

        sent(6, kv.at[:, 1, :, pl.ds(1, frames)])
        pltpu.make_async_copy(os, os, out_sem).wait()

    in_hbm = pl.BlockSpec(memory_space=pl.ANY)
    block = (half, cols, HD)
    return pl.pallas_call(
        kernel,
        out_shape=jax.ShapeDtypeStruct(queries.shape, queries.dtype),
        in_specs=[in_hbm] * 4,
        out_specs=pl.BlockSpec(memory_space=pl.ANY),
        scratch_shapes=[
            pltpu.SMEM(widths.shape, widths.dtype),
            pltpu.VMEM((heads, 2, frames) + block, jnp.bfloat16),
            pltpu.VMEM((heads, frames) + block, jnp.bfloat16),
            pltpu.VMEM((heads, 2, 2, 2 * frames) + block, jnp.bfloat16),
            pltpu.VMEM((heads, 2, 2 * frames) + block, jnp.bfloat16),
            pltpu.VMEM((2, heads, 2, 1) + block, jnp.bfloat16),
            pltpu.VMEM((heads, 2, quarter, HD), jnp.float32),
            pltpu.VMEM((heads, 8, quarter), jnp.float32),
            pltpu.VMEM((heads, frames) + block, jnp.bfloat16),
            pltpu.VMEM((heads, 8, quarter), jnp.float32),
            pltpu.VMEM((heads, frames) + block, jnp.bfloat16),
            pltpu.VMEM((heads, 8, quarter), jnp.float32),
            pltpu.VMEM((heads, frames, rows, cols, HD), jnp.bfloat16),
            pltpu.VMEM((2, pair, pair), jnp.float32),
            pltpu.SemaphoreType.DMA(()),
            pltpu.SemaphoreType.DMA((2, 3, heads)),
            pltpu.SemaphoreType.DMA(()),
            pltpu.SemaphoreType.DMA((10,)),
            pltpu.SemaphoreType.DMA((2, 2, heads)),
            pltpu.SemaphoreType.DMA((heads,)),
            pltpu.SemaphoreType.DMA((heads,)),
            pltpu.SemaphoreType.DMA((heads,)),
            pltpu.SemaphoreType.DMA((heads,)),
            pltpu.SemaphoreType.DMA((2, heads)),
            pltpu.SemaphoreType.DMA((2, heads)),
        ],
        compiler_params=pltpu.CompilerParams(
            collective_id=0, has_side_effects=True, vmem_limit_bytes=VMEM
        ),
    )(widths, queries, keys, values)


def solution(mesh):
    placed = P("tm", "height", None, None)
    return jax.shard_map(
        on_device,
        mesh=mesh,
        in_specs=(placed, placed, placed, P()),
        out_specs=placed,
        check_vma=False,
    )
```

```python
import math

import jax
import jax.numpy as jnp
from jax import lax
from jax.experimental import pallas as pl
from jax.experimental.pallas import tpu as pltpu
from jax.sharding import PartitionSpec as P

HD = 128
MESH = pl.DeviceIdType.MESH
X_AHEAD = 10
LAG = 2
SAME = ((0, 3, 6, 9), (0, 3, 6, 9))
SAME_INNER = ((), ())
SAME_OUTER = ((), ())
FAR = (tuple(range(10)), (1, 3, 5, 7))
PASS_AHEAD = 2
VMEM = 52 * 2**20


def on_device(queries, keys, values, widths):
    frames, rows, cols, feats = queries.shape
    heads = feats // HD
    half = rows // 2
    tm_count, height_count = lax.axis_size("tm"), lax.axis_size("height")
    frame_total = tm_count * frames
    quarter = half * cols
    pair = 2 * quarter
    factor = math.log2(math.e) / math.sqrt(HD)

    def kernel(
        w_hbm,
        q_ref,
        k_ref,
        v_ref,
        o_ref,
        w_ref,
        qs,
        qn,
        kv,
        sib,
        hold,
        part_o,
        part_l,
        send_o,
        send_l,
        got_o,
        got_l,
        os,
        bias,
        w_sem,
        local_sem,
        out_sem,
        send_sem,
        x_sem,
        q_sem,
        o_sem,
        l_sem,
        own_sem,
        fwd_sem,
        hold_sem,
    ):
        t, h = lax.axis_index("tm"), lax.axis_index("height")
        core = lax.rem(h, 2)
        far = h - 1 + 2 * core
        near = h + 1 - 2 * core
        has_far = (far >= 0) & (far < height_count)
        leads = has_far & ((core == 1) != (jnp.minimum(h, far) == height_count // 2 - 1))
        follows = has_far & jnp.logical_not(leads)
        first_row = (half * core, half * (1 - core))
        has_next, has_prev = t < tm_count - 1, t > 0
        mid = tm_count // 2
        ends = (0, tm_count - 1)
        is_mid = (t == mid - 1) | (t == mid)
        is_end = (t == 0) | (t == tm_count - 1)

        def lanes(g):
            return pl.ds(pl.multiple_of(g * HD, HD), HD)

        def local_kv(side, g):
            at = pl.ds(first_row[side], half)
            return tuple(
                pltpu.make_async_copy(
                    ref.at[:, at, :, lanes(g)],
                    kv.at[g, side, part, pl.ds(1, frames)],
                    local_sem.at[side, part, g],
                )
                for part, ref in enumerate((k_ref, v_ref))
            )

        def local_q(side, g):
            at = pl.ds(first_row[side], half)
            return pltpu.make_async_copy(
                q_ref.at[:, at, :, lanes(g)], qs.at[g, side], local_sem.at[side, 2, g]
            )

        def result(g):
            return pltpu.make_async_copy(os.at[g], o_ref.at[:, :, :, lanes(g)], out_sem)

        def remote(src, dst, send, recv, to):
            return pltpu.make_async_remote_copy(
                src_ref=src,
                dst_ref=dst,
                send_sem=send_sem.at[send],
                recv_sem=recv,
                device_id=to,
                device_id_type=MESH,
            )

        x_from, x_into = (2, 1), (0, 3)
        step_to = ((t + 1, h), (t - 1, h))
        x_sends, x_gets = (has_next, has_prev), (has_prev, has_next)
        detours = ((mid - 1, ends[1], mid), (mid, ends[0], mid - 1))
        turn = height_count // 2
        outer = (h < 2) | (h >= height_count - 2)
        inner_rows = (h >= turn - 2) & (h < turn + 2)
        other = lax.rem(h + turn, height_count)

        def x_copy(way, side, g):
            return remote(
                kv.at[g, side, :, pl.ds(x_from[way], 1)],
                kv.at[g, side, :, pl.ds(x_into[way], 1)],
                way,
                x_sem.at[way, side, g],
                step_to[way],
            )

        def first_leg(way, side, g, row, plane):
            return remote(
                kv.at[g, side, :, pl.ds(x_from[way], 1)],
                hold.at[plane, g],
                way,
                hold_sem.at[plane, g],
                (detours[way][1], row),
            )

        def second_leg(way, side, g, row, plane):
            return remote(
                hold.at[plane, g],
                kv.at[g, side, :, pl.ds(x_into[way], 1)],
                (2, 9, 10, 11)[plane],
                x_sem.at[way, side, g],
                (detours[way][2], row),
            )

        def among(g, chosen):
            found = jnp.bool_(False)
            for one in chosen:
                found = found | (g == one)
            return found

        def goes_round(side, g):
            turns = jnp.logical_not(outer | inner_rows) & among(g, SAME[side])
            turns = turns | (inner_rows & among(g, SAME_INNER[side]))
            return turns | (outer & among(g, SAME_OUTER[side]))

        def goes_far(side, g):
            return among(g, FAR[side])

        def begin_x(side, g):
            for copy in local_kv(side, g):
                copy.wait()
            for way in range(2):
                round_trip = (t == detours[way][0]) & goes_round(side, g)

                @pl.when(round_trip)
                def _():
                    first_leg(way, side, g, h, side).start()

                direct = x_sends[way] & jnp.logical_not(round_trip)
                far_trip = (t == detours[way][0]) & outer & goes_far(side, g)

                @pl.when(far_trip)
                def _():
                    first_leg(way, side, g, other, 2 + side).start()

                direct = direct & jnp.logical_not(far_trip)

                @pl.when(direct)
                def _():
                    x_copy(way, side, g).start()

        def begin_step(step):
            @pl.when(step < heads)
            def _():
                begin_x(0, step)

            @pl.when((step >= heads) & (step < 2 * heads))
            def _():
                begin_x(1, step - heads)

        def arrive_x(way, side, g):
            @pl.when(x_gets[way])
            def _():
                x_copy(way, side, g).wait_recv()

        def pass_on(side, g):
            for way in range(2):

                @pl.when((t == detours[way][1]) & goes_round(side, g))
                def _():
                    first_leg(way, side, g, h, side).wait_recv()
                    second_leg(way, side, g, h, side).start()

                @pl.when((t == detours[way][1]) & inner_rows & goes_far(side, g))
                def _():
                    first_leg(way, side, g, other, 2 + side).wait_recv()
                    second_leg(way, side, g, other, 2 + side).start()

        def q_copy(g):
            return remote(qs.at[g, 0], qn.at[g], 3, q_sem.at[g], (t, far))

        def o_copy(g):
            return remote(send_o.at[g], got_o.at[g], 4, o_sem.at[g], (t, far))

        def l_copy(g):
            return remote(send_l.at[g], got_l.at[g], 5, l_sem.at[g], (t, far))

        def own_copy(g):
            return remote(
                kv.at[g, 1, :, pl.ds(1, frames)],
                sib.at[g, :, pl.ds(1, frames)],
                6,
                own_sem.at[g],
                (t, near),
            )

        def fwd_copy(way, g):
            return remote(
                kv.at[g, 1, :, pl.ds(x_into[way], 1)],
                sib.at[g, :, pl.ds(x_into[way], 1)],
                7 + way,
                fwd_sem.at[way, g],
                (t, near),
            )

        def begin_q(g):
            local_q(0, g).wait()
            q_copy(g).start()

        barrier = pltpu.get_barrier_semaphore()
        greeted = [(has_next, (t + 1, h)), (has_prev, (t - 1, h))]
        greeted += [(is_mid, (at, h)) for at in ends]
        greeted += [(is_end, (at, h)) for at in (mid - 1, mid)]
        greeted += [(is_mid & outer, (at, other)) for at in ends]
        greeted += [(is_end & inner_rows, (at, other)) for at in (mid - 1, mid)]
        total = jnp.int32(1)
        pl.semaphore_signal(barrier, inc=1, device_id=(t, near), device_id_type=MESH)
        for present, place in greeted:
            total = total + present.astype(jnp.int32)

            @pl.when(present)
            def _():
                pl.semaphore_signal(barrier, inc=1, device_id=place, device_id_type=MESH)

        total = total + follows.astype(jnp.int32)

        @pl.when(leads)
        def _():
            pl.semaphore_signal(barrier, inc=1, device_id=(t, far), device_id_type=MESH)

        @pl.loop(0, heads)
        def _(g):
            for copy in local_kv(0, g):
                copy.start()

        sizes = pltpu.make_async_copy(w_hbm, w_ref, w_sem)
        sizes.start()

        @pl.loop(0, heads)
        def _(g):
            local_q(0, g).start()

        pl.semaphore_wait(barrier, total)

        @pl.loop(0, min(X_AHEAD, heads))
        def _(g):
            begin_x(0, g)

        @pl.when(follows)
        def _():
            @pl.loop(0, heads)
            def _(g):
                begin_q(g)

        @pl.loop(0, heads)
        def _(g):
            for copy in local_kv(1, g):
                copy.start()
            local_q(1, g).start()

        @pl.loop(heads, max(X_AHEAD, heads))
        def _(g):
            begin_step(g)

        for present, at in ((has_prev, 0), (has_next, 3)):

            @pl.when(jnp.logical_not(present))
            def _():
                @pl.loop(0, heads)
                def _(g):
                    for part in range(2):
                        for block in (kv.at[g, 0, part, at], kv.at[g, 1, part, at]):
                            block[...] = jnp.zeros(block.shape, block.dtype)
                        sib[g, part, at] = jnp.zeros((half, cols, HD), sib.dtype)

        @pl.when(jnp.logical_not(has_far))
        def _():
            @pl.loop(0, heads)
            def _(g):
                qn[g] = jnp.zeros(qn.shape[1:], qn.dtype)
                got_o[g] = jnp.zeros(got_o.shape[1:], got_o.dtype)
                got_l[g] = jnp.full(got_l.shape[1:], -1e30, got_l.dtype)

        sizes.wait()
        key = lax.broadcasted_iota(jnp.int32, (pair, pair), 1)
        query = lax.broadcasted_iota(jnp.int32, (pair, pair), 0)
        for a in range(2):
            size = []
            for frame in (t * frames - 1 + 2 * a, t * frames + 2 * a):
                inside = (frame >= 0) & (frame < frame_total)
                width = w_ref[jnp.clip(frame, 0, frame_total - 1)]
                size.append(jnp.where(inside, width, 0))
            width = jnp.where(key < quarter, size[0], size[1])
            same = (query < quarter) & (key == query + (1 - a) * quarter)
            ok = (key % cols < width) | same
            bias[a] = jnp.where(ok, 0.0, -1e30).astype(jnp.float32)

        eye = lax.broadcasted_iota(jnp.int32, (quarter, quarter), 0) == (
            lax.broadcasted_iota(jnp.int32, (quarter, quarter), 1)
        )

        def to_row(column):
            return jnp.sum(jnp.where(eye, column, 0.0), axis=0, keepdims=True)

        def to_column(row):
            return jnp.sum(jnp.where(eye, row, 0.0), axis=1, keepdims=True)

        def inner(x, y):
            return lax.dot_general(
                x, y, (((1,), (1,)), ((), ())), preferred_element_type=jnp.float32
            )

        first = lax.broadcasted_iota(jnp.int32, (8, quarter), 0) == 0

        def shares(g):
            logs = []
            for a in range(2):
                q = jnp.concatenate(
                    [qs[g, 0, a].reshape(quarter, HD), qn[g, a].reshape(quarter, HD)], axis=0
                )
                k = kv[g, 0, 0, pl.ds(2 * a, 2)].reshape(pair, HD)
                v = kv[g, 0, 1, pl.ds(2 * a, 2)].reshape(pair, HD)
                s = inner(q, k) + bias[a]
                top = jnp.max(s, axis=1, keepdims=True)
                p = jnp.exp2((s - top) * factor)
                total = jnp.sum(p, axis=1, keepdims=True)
                out = jnp.dot(p.astype(jnp.bfloat16), v, preferred_element_type=jnp.float32)
                out = out * (1.0 / total)
                logs.append(top * factor + jnp.log2(total))
                part_o[g, a] = out[:quarter]
                send_o[g, a] = out[quarter:].astype(jnp.bfloat16).reshape(half, cols, HD)
            part_l[g] = jnp.where(first, to_row(logs[0][:quarter]), to_row(logs[1][:quarter]))
            send_l[g] = jnp.where(first, to_row(logs[0][quarter:]), to_row(logs[1][quarter:]))

        def merge(g):
            @pl.when(has_far)
            def _():
                o_copy(g).wait_recv()
                l_copy(g).wait_recv()

            weight = 1.0 / (1.0 + jnp.exp2(got_l[g] - part_l[g]))
            for a in range(2):
                mine = to_column(weight[a : a + 1])
                other = got_o[g, a].reshape(quarter, HD).astype(jnp.float32)
                out = other + mine * (part_o[g, a] - other)
                os[g, a, pl.ds(first_row[0], half)] = out.astype(jnp.bfloat16).reshape(
                    half, cols, HD
                )

        def whole(g):
            local_q(1, g).wait()
            own_copy(g).wait_recv()
            for way in range(2):

                @pl.when(x_gets[way])
                def _():
                    fwd_copy(way, g).wait_recv()

            for a in range(2):
                q = qs[g, 1, a].reshape(quarter, HD)
                at = pl.ds(2 * a, 2)
                s1 = inner(q, kv[g, 1, 0, at].reshape(pair, HD)) + bias[a, pl.ds(0, quarter)]
                s2 = inner(q, sib[g, 0, at].reshape(pair, HD)) + bias[a, pl.ds(quarter, quarter)]
                top = jnp.maximum(
                    jnp.max(s1, axis=1, keepdims=True), jnp.max(s2, axis=1, keepdims=True)
                )
                p1 = jnp.exp2((s1 - top) * factor)
                p2 = jnp.exp2((s2 - top) * factor)
                total = jnp.sum(p1, axis=1, keepdims=True) + jnp.sum(p2, axis=1, keepdims=True)
                v1 = kv[g, 1, 1, at].reshape(pair, HD)
                v2 = sib[g, 1, at].reshape(pair, HD)
                out = jnp.dot(p1.astype(jnp.bfloat16), v1, preferred_element_type=jnp.float32)
                out += jnp.dot(p2.astype(jnp.bfloat16), v2, preferred_element_type=jnp.float32)
                out = out * (1.0 / total)
                os[g, a, pl.ds(first_row[1], half)] = out.astype(jnp.bfloat16).reshape(
                    half, cols, HD
                )

        @pl.loop(0, PASS_AHEAD)
        def _(g):
            pass_on(0, g)

        def pass_step(step):
            @pl.when(step < heads)
            def _():
                pass_on(0, step)

            @pl.when((step >= heads) & (step < 2 * heads))
            def _():
                pass_on(1, step - heads)

        @pl.loop(0, heads)
        def _(g):
            pass_step(g + PASS_AHEAD)
            arrive_x(0, 0, g)
            arrive_x(1, 0, g)
            begin_step(g + X_AHEAD)

            @pl.when(has_far)
            def _():
                q_copy(g).wait_recv()

            @pl.when(leads & (g == 0))
            def _():
                @pl.loop(0, heads)
                def _(i):
                    begin_q(i)

            @pl.when(jnp.logical_not(has_far))
            def _():
                local_q(0, g).wait()

            shares(g)

            @pl.when(has_far)
            def _():
                o_copy(g).start()
                l_copy(g).start()

        @pl.loop(0, heads + LAG)
        def _(g):
            @pl.when(g >= LAG)
            def _():
                merge(g - LAG)
                whole(g - LAG)
                result(g - LAG).start()

            @pl.when(g < heads)
            def _():
                own_copy(g).start()
                pass_step(heads + g + PASS_AHEAD)
                for way in range(2):
                    arrive_x(way, 1, g)

                    @pl.when(x_gets[way])
                    def _():
                        fwd_copy(way, g).start()

                begin_step(heads + g + X_AHEAD)

        def sent(index, ref):
            remote(ref, ref, index, hold_sem.at[0, 0], (t, near)).wait_send()

        for way in range(2):

            @pl.when(x_sends[way])
            def _():
                sent(way, kv.at[:, :, :, pl.ds(x_from[way], 1)])

            @pl.when(x_gets[way])
            def _():
                sent(7 + way, kv.at[:, 1, :, pl.ds(x_into[way], 1)])

        for side, index in ((0, 2), (1, 9)):
            for rows_here, chosen in (
                (jnp.logical_not(outer | inner_rows), SAME[side]),
                (inner_rows, SAME_INNER[side]),
                (outer, SAME_OUTER[side]),
            ):
                if chosen:

                    @pl.when(is_end & rows_here)
                    def _():
                        sent(index, hold.at[side, pl.ds(0, len(chosen))])

            if FAR[side]:

                @pl.when(is_end & inner_rows)
                def _():
                    sent(10 + side, hold.at[2 + side, pl.ds(0, len(FAR[side]))])

        @pl.when(has_far)
        def _():
            sent(3, qn)
            sent(4, send_o)
            sent(5, send_l)

        sent(6, kv.at[:, 1, :, pl.ds(1, frames)])
        pltpu.make_async_copy(os, os, out_sem).wait()

    in_hbm = pl.BlockSpec(memory_space=pl.ANY)
    block = (half, cols, HD)
    return pl.pallas_call(
        kernel,
        out_shape=jax.ShapeDtypeStruct(queries.shape, queries.dtype),
        in_specs=[in_hbm] * 4,
        out_specs=pl.BlockSpec(memory_space=pl.ANY),
        scratch_shapes=[
            pltpu.SMEM(widths.shape, widths.dtype),
            pltpu.VMEM((heads, 2, frames) + block, jnp.bfloat16),
            pltpu.VMEM((heads, frames) + block, jnp.bfloat16),
            pltpu.VMEM((heads, 2, 2, 2 * frames) + block, jnp.bfloat16),
            pltpu.VMEM((heads, 2, 2 * frames) + block, jnp.bfloat16),
            pltpu.VMEM((4, heads, 2, 1) + block, jnp.bfloat16),
            pltpu.VMEM((heads, 2, quarter, HD), jnp.float32),
            pltpu.VMEM((heads, 8, quarter), jnp.float32),
            pltpu.VMEM((heads, frames) + block, jnp.bfloat16),
            pltpu.VMEM((heads, 8, quarter), jnp.float32),
            pltpu.VMEM((heads, frames) + block, jnp.bfloat16),
            pltpu.VMEM((heads, 8, quarter), jnp.float32),
            pltpu.VMEM((heads, frames, rows, cols, HD), jnp.bfloat16),
            pltpu.VMEM((2, pair, pair), jnp.float32),
            pltpu.SemaphoreType.DMA(()),
            pltpu.SemaphoreType.DMA((2, 3, heads)),
            pltpu.SemaphoreType.DMA(()),
            pltpu.SemaphoreType.DMA((12,)),
            pltpu.SemaphoreType.DMA((2, 2, heads)),
            pltpu.SemaphoreType.DMA((heads,)),
            pltpu.SemaphoreType.DMA((heads,)),
            pltpu.SemaphoreType.DMA((heads,)),
            pltpu.SemaphoreType.DMA((heads,)),
            pltpu.SemaphoreType.DMA((2, heads)),
            pltpu.SemaphoreType.DMA((4, heads)),
        ],
        compiler_params=pltpu.CompilerParams(
            collective_id=0, has_side_effects=True, vmem_limit_bytes=VMEM
        ),
    )(widths, queries, keys, values)


def solution(mesh):
    placed = P("tm", "height", None, None)
    return jax.shard_map(
        on_device,
        mesh=mesh,
        in_specs=(placed, placed, placed, P()),
        out_specs=placed,
        check_vma=False,
    )
```

```python
import math

import jax
import jax.numpy as jnp
from jax import lax
from jax.experimental import pallas as pl
from jax.experimental.pallas import tpu as pltpu
from jax.sharding import PartitionSpec as P

HD = 128
MESH = pl.DeviceIdType.MESH
X_AHEAD = 10
LAG = 2
SAME = ((0, 3, 6, 9), (0, 3, 6, 9))
SAME_INNER = ((), ())
SAME_OUTER = ((), ())
FAR = (tuple(range(9)), (1, 3, 5, 7))
PASS_AHEAD = 2
VMEM = 52 * 2**20


def on_device(queries, keys, values, widths):
    frames, rows, cols, feats = queries.shape
    heads = feats // HD
    half = rows // 2
    tm_count, height_count = lax.axis_size("tm"), lax.axis_size("height")
    frame_total = tm_count * frames
    quarter = half * cols
    pair = 2 * quarter
    factor = math.log2(math.e) / math.sqrt(HD)

    def kernel(
        w_hbm,
        q_ref,
        k_ref,
        v_ref,
        o_ref,
        w_ref,
        qs,
        qn,
        kv,
        sib,
        hold,
        part_o,
        part_l,
        send_o,
        send_l,
        got_o,
        got_l,
        os,
        bias,
        w_sem,
        local_sem,
        out_sem,
        send_sem,
        x_sem,
        q_sem,
        o_sem,
        l_sem,
        own_sem,
        fwd_sem,
        hold_sem,
    ):
        t, h = lax.axis_index("tm"), lax.axis_index("height")
        core = lax.rem(h, 2)
        far = h - 1 + 2 * core
        near = h + 1 - 2 * core
        has_far = (far >= 0) & (far < height_count)
        leads = has_far & ((core == 1) != (jnp.minimum(h, far) == height_count // 2 - 1))
        follows = has_far & jnp.logical_not(leads)
        first_row = (half * core, half * (1 - core))
        has_next, has_prev = t < tm_count - 1, t > 0
        mid = tm_count // 2
        ends = (0, tm_count - 1)
        is_mid = (t == mid - 1) | (t == mid)
        is_end = (t == 0) | (t == tm_count - 1)

        def lanes(g):
            return pl.ds(pl.multiple_of(g * HD, HD), HD)

        def local_kv(side, g):
            at = pl.ds(first_row[side], half)
            return tuple(
                pltpu.make_async_copy(
                    ref.at[:, at, :, lanes(g)],
                    kv.at[g, side, part, pl.ds(1, frames)],
                    local_sem.at[side, part, g],
                )
                for part, ref in enumerate((k_ref, v_ref))
            )

        def local_q(side, g):
            at = pl.ds(first_row[side], half)
            return pltpu.make_async_copy(
                q_ref.at[:, at, :, lanes(g)], qs.at[g, side], local_sem.at[side, 2, g]
            )

        def result(g):
            return pltpu.make_async_copy(os.at[g], o_ref.at[:, :, :, lanes(g)], out_sem)

        def remote(src, dst, send, recv, to):
            return pltpu.make_async_remote_copy(
                src_ref=src,
                dst_ref=dst,
                send_sem=send_sem.at[send],
                recv_sem=recv,
                device_id=to,
                device_id_type=MESH,
            )

        x_from, x_into = (2, 1), (0, 3)
        step_to = ((t + 1, h), (t - 1, h))
        x_sends, x_gets = (has_next, has_prev), (has_prev, has_next)
        detours = ((mid - 1, ends[1], mid), (mid, ends[0], mid - 1))
        turn = height_count // 2
        outer = (h < 2) | (h >= height_count - 2)
        inner_rows = (h >= turn - 2) & (h < turn + 2)
        other = lax.rem(h + turn, height_count)

        def x_copy(way, side, g):
            return remote(
                kv.at[g, side, :, pl.ds(x_from[way], 1)],
                kv.at[g, side, :, pl.ds(x_into[way], 1)],
                way,
                x_sem.at[way, side, g],
                step_to[way],
            )

        def first_leg(way, side, g, row, plane):
            return remote(
                kv.at[g, side, :, pl.ds(x_from[way], 1)],
                hold.at[plane, g],
                way,
                hold_sem.at[plane, g],
                (detours[way][1], row),
            )

        def second_leg(way, side, g, row, plane):
            return remote(
                hold.at[plane, g],
                kv.at[g, side, :, pl.ds(x_into[way], 1)],
                (2, 9, 10, 11)[plane],
                x_sem.at[way, side, g],
                (detours[way][2], row),
            )

        def among(g, chosen):
            found = jnp.bool_(False)
            for one in chosen:
                found = found | (g == one)
            return found

        def goes_round(side, g):
            turns = jnp.logical_not(outer | inner_rows) & among(g, SAME[side])
            turns = turns | (inner_rows & among(g, SAME_INNER[side]))
            return turns | (outer & among(g, SAME_OUTER[side]))

        def goes_far(side, g):
            return among(g, FAR[side])

        def begin_x(side, g):
            for copy in local_kv(side, g):
                copy.wait()
            for way in range(2):
                round_trip = (t == detours[way][0]) & goes_round(side, g)

                @pl.when(round_trip)
                def _():
                    first_leg(way, side, g, h, side).start()

                direct = x_sends[way] & jnp.logical_not(round_trip)
                far_trip = (t == detours[way][0]) & outer & goes_far(side, g)

                @pl.when(far_trip)
                def _():
                    first_leg(way, side, g, other, 2 + side).start()

                direct = direct & jnp.logical_not(far_trip)

                @pl.when(direct)
                def _():
                    x_copy(way, side, g).start()

        def begin_step(step):
            @pl.when(step < heads)
            def _():
                begin_x(0, step)

            @pl.when((step >= heads) & (step < 2 * heads))
            def _():
                begin_x(1, step - heads)

        def arrive_x(way, side, g):
            @pl.when(x_gets[way])
            def _():
                x_copy(way, side, g).wait_recv()

        def pass_on(side, g):
            for way in range(2):

                @pl.when((t == detours[way][1]) & goes_round(side, g))
                def _():
                    first_leg(way, side, g, h, side).wait_recv()
                    second_leg(way, side, g, h, side).start()

                @pl.when((t == detours[way][1]) & inner_rows & goes_far(side, g))
                def _():
                    first_leg(way, side, g, other, 2 + side).wait_recv()
                    second_leg(way, side, g, other, 2 + side).start()

        def q_copy(g):
            return remote(qs.at[g, 0], qn.at[g], 3, q_sem.at[g], (t, far))

        def o_copy(g):
            return remote(send_o.at[g], got_o.at[g], 4, o_sem.at[g], (t, far))

        def l_copy(g):
            return remote(send_l.at[g], got_l.at[g], 5, l_sem.at[g], (t, far))

        def own_copy(g):
            return remote(
                kv.at[g, 1, :, pl.ds(1, frames)],
                sib.at[g, :, pl.ds(1, frames)],
                6,
                own_sem.at[g],
                (t, near),
            )

        def fwd_copy(way, g):
            return remote(
                kv.at[g, 1, :, pl.ds(x_into[way], 1)],
                sib.at[g, :, pl.ds(x_into[way], 1)],
                7 + way,
                fwd_sem.at[way, g],
                (t, near),
            )

        def begin_q(g):
            local_q(0, g).wait()
            q_copy(g).start()

        barrier = pltpu.get_barrier_semaphore()
        greeted = [(has_next, (t + 1, h)), (has_prev, (t - 1, h))]
        greeted += [(is_mid, (at, h)) for at in ends]
        greeted += [(is_end, (at, h)) for at in (mid - 1, mid)]
        greeted += [(is_mid & outer, (at, other)) for at in ends]
        greeted += [(is_end & inner_rows, (at, other)) for at in (mid - 1, mid)]
        total = jnp.int32(1)
        pl.semaphore_signal(barrier, inc=1, device_id=(t, near), device_id_type=MESH)
        for present, place in greeted:
            total = total + present.astype(jnp.int32)

            @pl.when(present)
            def _():
                pl.semaphore_signal(barrier, inc=1, device_id=place, device_id_type=MESH)

        total = total + follows.astype(jnp.int32)

        @pl.when(leads)
        def _():
            pl.semaphore_signal(barrier, inc=1, device_id=(t, far), device_id_type=MESH)

        @pl.loop(0, heads)
        def _(g):
            for copy in local_kv(0, g):
                copy.start()

        sizes = pltpu.make_async_copy(w_hbm, w_ref, w_sem)
        sizes.start()

        @pl.loop(0, heads)
        def _(g):
            local_q(0, g).start()

        pl.semaphore_wait(barrier, total)

        @pl.loop(0, min(X_AHEAD, heads))
        def _(g):
            begin_x(0, g)

        @pl.when(follows)
        def _():
            @pl.loop(0, heads)
            def _(g):
                begin_q(g)

        @pl.loop(0, heads)
        def _(g):
            for copy in local_kv(1, g):
                copy.start()
            local_q(1, g).start()

        @pl.loop(heads, max(X_AHEAD, heads))
        def _(g):
            begin_step(g)

        for present, at in ((has_prev, 0), (has_next, 3)):

            @pl.when(jnp.logical_not(present))
            def _():
                @pl.loop(0, heads)
                def _(g):
                    for part in range(2):
                        for block in (kv.at[g, 0, part, at], kv.at[g, 1, part, at]):
                            block[...] = jnp.zeros(block.shape, block.dtype)
                        sib[g, part, at] = jnp.zeros((half, cols, HD), sib.dtype)

        @pl.when(jnp.logical_not(has_far))
        def _():
            @pl.loop(0, heads)
            def _(g):
                qn[g] = jnp.zeros(qn.shape[1:], qn.dtype)
                got_o[g] = jnp.zeros(got_o.shape[1:], got_o.dtype)
                got_l[g] = jnp.full(got_l.shape[1:], -1e30, got_l.dtype)

        sizes.wait()
        key = lax.broadcasted_iota(jnp.int32, (pair, pair), 1)
        query = lax.broadcasted_iota(jnp.int32, (pair, pair), 0)
        for a in range(2):
            size = []
            for frame in (t * frames - 1 + 2 * a, t * frames + 2 * a):
                inside = (frame >= 0) & (frame < frame_total)
                width = w_ref[jnp.clip(frame, 0, frame_total - 1)]
                size.append(jnp.where(inside, width, 0))
            width = jnp.where(key < quarter, size[0], size[1])
            same = (query < quarter) & (key == query + (1 - a) * quarter)
            ok = (key % cols < width) | same
            bias[a] = jnp.where(ok, 0.0, -1e30).astype(jnp.float32)

        eye = lax.broadcasted_iota(jnp.int32, (quarter, quarter), 0) == (
            lax.broadcasted_iota(jnp.int32, (quarter, quarter), 1)
        )

        def to_row(column):
            return jnp.sum(jnp.where(eye, column, 0.0), axis=0, keepdims=True)

        def to_column(row):
            return jnp.sum(jnp.where(eye, row, 0.0), axis=1, keepdims=True)

        def inner(x, y):
            return lax.dot_general(
                x, y, (((1,), (1,)), ((), ())), preferred_element_type=jnp.float32
            )

        first = lax.broadcasted_iota(jnp.int32, (8, quarter), 0) == 0

        def shares(g):
            logs = []
            for a in range(2):
                q = jnp.concatenate(
                    [qs[g, 0, a].reshape(quarter, HD), qn[g, a].reshape(quarter, HD)], axis=0
                )
                k = kv[g, 0, 0, pl.ds(2 * a, 2)].reshape(pair, HD)
                v = kv[g, 0, 1, pl.ds(2 * a, 2)].reshape(pair, HD)
                s = inner(q, k) + bias[a]
                top = jnp.max(s, axis=1, keepdims=True)
                p = jnp.exp2((s - top) * factor)
                total = jnp.sum(p, axis=1, keepdims=True)
                out = jnp.dot(p.astype(jnp.bfloat16), v, preferred_element_type=jnp.float32)
                out = out * (1.0 / total)
                logs.append(top * factor + jnp.log2(total))
                part_o[g, a] = out[:quarter]
                send_o[g, a] = out[quarter:].astype(jnp.bfloat16).reshape(half, cols, HD)
            part_l[g] = jnp.where(first, to_row(logs[0][:quarter]), to_row(logs[1][:quarter]))
            send_l[g] = jnp.where(first, to_row(logs[0][quarter:]), to_row(logs[1][quarter:]))

        def merge(g):
            @pl.when(has_far)
            def _():
                o_copy(g).wait_recv()
                l_copy(g).wait_recv()

            weight = 1.0 / (1.0 + jnp.exp2(got_l[g] - part_l[g]))
            for a in range(2):
                mine = to_column(weight[a : a + 1])
                other = got_o[g, a].reshape(quarter, HD).astype(jnp.float32)
                out = other + mine * (part_o[g, a] - other)
                os[g, a, pl.ds(first_row[0], half)] = out.astype(jnp.bfloat16).reshape(
                    half, cols, HD
                )

        def whole(g):
            local_q(1, g).wait()
            own_copy(g).wait_recv()
            for way in range(2):

                @pl.when(x_gets[way])
                def _():
                    fwd_copy(way, g).wait_recv()

            for a in range(2):
                q = qs[g, 1, a].reshape(quarter, HD)
                at = pl.ds(2 * a, 2)
                s1 = inner(q, kv[g, 1, 0, at].reshape(pair, HD)) + bias[a, pl.ds(0, quarter)]
                s2 = inner(q, sib[g, 0, at].reshape(pair, HD)) + bias[a, pl.ds(quarter, quarter)]
                top = jnp.maximum(
                    jnp.max(s1, axis=1, keepdims=True), jnp.max(s2, axis=1, keepdims=True)
                )
                p1 = jnp.exp2((s1 - top) * factor)
                p2 = jnp.exp2((s2 - top) * factor)
                total = jnp.sum(p1, axis=1, keepdims=True) + jnp.sum(p2, axis=1, keepdims=True)
                v1 = kv[g, 1, 1, at].reshape(pair, HD)
                v2 = sib[g, 1, at].reshape(pair, HD)
                out = jnp.dot(p1.astype(jnp.bfloat16), v1, preferred_element_type=jnp.float32)
                out += jnp.dot(p2.astype(jnp.bfloat16), v2, preferred_element_type=jnp.float32)
                out = out * (1.0 / total)
                os[g, a, pl.ds(first_row[1], half)] = out.astype(jnp.bfloat16).reshape(
                    half, cols, HD
                )

        @pl.loop(0, PASS_AHEAD)
        def _(g):
            pass_on(0, g)

        def pass_step(step):
            @pl.when(step < heads)
            def _():
                pass_on(0, step)

            @pl.when((step >= heads) & (step < 2 * heads))
            def _():
                pass_on(1, step - heads)

        @pl.loop(0, heads)
        def _(g):
            pass_step(g + PASS_AHEAD)
            arrive_x(0, 0, g)
            arrive_x(1, 0, g)
            begin_step(g + X_AHEAD)

            @pl.when(has_far)
            def _():
                q_copy(g).wait_recv()

            @pl.when(leads & (g == 0))
            def _():
                @pl.loop(0, heads)
                def _(i):
                    begin_q(i)

            @pl.when(jnp.logical_not(has_far))
            def _():
                local_q(0, g).wait()

            shares(g)

            @pl.when(has_far)
            def _():
                o_copy(g).start()
                l_copy(g).start()

        @pl.loop(0, heads + LAG)
        def _(g):
            @pl.when(g >= LAG)
            def _():
                merge(g - LAG)
                whole(g - LAG)
                result(g - LAG).start()

            @pl.when(g < heads)
            def _():
                own_copy(g).start()
                pass_step(heads + g + PASS_AHEAD)
                for way in range(2):
                    arrive_x(way, 1, g)

                    @pl.when(x_gets[way])
                    def _():
                        fwd_copy(way, g).start()

                begin_step(heads + g + X_AHEAD)

        def sent(index, ref):
            remote(ref, ref, index, hold_sem.at[0, 0], (t, near)).wait_send()

        for way in range(2):

            @pl.when(x_sends[way])
            def _():
                sent(way, kv.at[:, :, :, pl.ds(x_from[way], 1)])

            @pl.when(x_gets[way])
            def _():
                sent(7 + way, kv.at[:, 1, :, pl.ds(x_into[way], 1)])

        for side, index in ((0, 2), (1, 9)):
            for rows_here, chosen in (
                (jnp.logical_not(outer | inner_rows), SAME[side]),
                (inner_rows, SAME_INNER[side]),
                (outer, SAME_OUTER[side]),
            ):
                if chosen:

                    @pl.when(is_end & rows_here)
                    def _():
                        sent(index, hold.at[side, pl.ds(0, len(chosen))])

            if FAR[side]:

                @pl.when(is_end & inner_rows)
                def _():
                    sent(10 + side, hold.at[2 + side, pl.ds(0, len(FAR[side]))])

        @pl.when(has_far)
        def _():
            sent(3, qn)
            sent(4, send_o)
            sent(5, send_l)

        sent(6, kv.at[:, 1, :, pl.ds(1, frames)])
        pltpu.make_async_copy(os, os, out_sem).wait()

    in_hbm = pl.BlockSpec(memory_space=pl.ANY)
    block = (half, cols, HD)
    return pl.pallas_call(
        kernel,
        out_shape=jax.ShapeDtypeStruct(queries.shape, queries.dtype),
        in_specs=[in_hbm] * 4,
        out_specs=pl.BlockSpec(memory_space=pl.ANY),
        scratch_shapes=[
            pltpu.SMEM(widths.shape, widths.dtype),
            pltpu.VMEM((heads, 2, frames) + block, jnp.bfloat16),
            pltpu.VMEM((heads, frames) + block, jnp.bfloat16),
            pltpu.VMEM((heads, 2, 2, 2 * frames) + block, jnp.bfloat16),
            pltpu.VMEM((heads, 2, 2 * frames) + block, jnp.bfloat16),
            pltpu.VMEM((4, heads, 2, 1) + block, jnp.bfloat16),
            pltpu.VMEM((heads, 2, quarter, HD), jnp.float32),
            pltpu.VMEM((heads, 8, quarter), jnp.float32),
            pltpu.VMEM((heads, frames) + block, jnp.bfloat16),
            pltpu.VMEM((heads, 8, quarter), jnp.float32),
            pltpu.VMEM((heads, frames) + block, jnp.bfloat16),
            pltpu.VMEM((heads, 8, quarter), jnp.float32),
            pltpu.VMEM((heads, frames, rows, cols, HD), jnp.bfloat16),
            pltpu.VMEM((2, pair, pair), jnp.float32),
            pltpu.SemaphoreType.DMA(()),
            pltpu.SemaphoreType.DMA((2, 3, heads)),
            pltpu.SemaphoreType.DMA(()),
            pltpu.SemaphoreType.DMA((12,)),
            pltpu.SemaphoreType.DMA((2, 2, heads)),
            pltpu.SemaphoreType.DMA((heads,)),
            pltpu.SemaphoreType.DMA((heads,)),
            pltpu.SemaphoreType.DMA((heads,)),
            pltpu.SemaphoreType.DMA((heads,)),
            pltpu.SemaphoreType.DMA((2, heads)),
            pltpu.SemaphoreType.DMA((4, heads)),
        ],
        compiler_params=pltpu.CompilerParams(
            collective_id=0, has_side_effects=True, vmem_limit_bytes=VMEM
        ),
    )(widths, queries, keys, values)


def solution(mesh):
    placed = P("tm", "height", None, None)
    return jax.shard_map(
        on_device,
        mesh=mesh,
        in_specs=(placed, placed, placed, P()),
        out_specs=placed,
        check_vma=False,
    )
```

```python
import math

import jax
import jax.numpy as jnp
from jax import lax
from jax.experimental import pallas as pl
from jax.experimental.pallas import tpu as pltpu
from jax.sharding import PartitionSpec as P

HD = 128
MESH = pl.DeviceIdType.MESH
X_AHEAD = 10
LAG = 2
SAME = ((0, 3, 6, 9), (0, 3, 6, 9))
SAME_INNER = ((), ())
SAME_OUTER = ((), ())
FAR = (tuple(range(9)), (1, 3, 5, 7))
PASS_AHEAD = 2
VMEM = 52 * 2**20


def on_device(queries, keys, values, widths):
    frames, rows, cols, feats = queries.shape
    heads = feats // HD
    half = rows // 2
    tm_count, height_count = lax.axis_size("tm"), lax.axis_size("height")
    frame_total = tm_count * frames
    quarter = half * cols
    pair = 2 * quarter
    factor = math.log2(math.e) / math.sqrt(HD)

    def kernel(
        w_hbm,
        q_ref,
        k_ref,
        v_ref,
        o_ref,
        w_ref,
        qs,
        qn,
        kv,
        sib,
        hold,
        part_o,
        part_l,
        send_o,
        send_l,
        got_o,
        got_l,
        os,
        bias,
        w_sem,
        local_sem,
        out_sem,
        send_sem,
        x_sem,
        q_sem,
        o_sem,
        l_sem,
        own_sem,
        fwd_sem,
        hold_sem,
    ):
        t, h = lax.axis_index("tm"), lax.axis_index("height")
        core = lax.rem(h, 2)
        far = h - 1 + 2 * core
        near = h + 1 - 2 * core
        has_far = (far >= 0) & (far < height_count)
        leads = has_far & ((core == 1) != (jnp.minimum(h, far) == height_count // 2 - 1))
        follows = has_far & jnp.logical_not(leads)
        first_row = (half * core, half * (1 - core))
        has_next, has_prev = t < tm_count - 1, t > 0
        mid = tm_count // 2
        ends = (0, tm_count - 1)
        is_mid = (t == mid - 1) | (t == mid)
        is_end = (t == 0) | (t == tm_count - 1)

        def lanes(g):
            return pl.ds(pl.multiple_of(g * HD, HD), HD)

        def local_kv(side, g):
            at = pl.ds(first_row[side], half)
            return tuple(
                pltpu.make_async_copy(
                    ref.at[:, at, :, lanes(g)],
                    kv.at[g, side, part, pl.ds(1, frames)],
                    local_sem.at[side, part, g],
                )
                for part, ref in enumerate((k_ref, v_ref))
            )

        def local_q(side, g):
            at = pl.ds(first_row[side], half)
            return pltpu.make_async_copy(
                q_ref.at[:, at, :, lanes(g)], qs.at[g, side], local_sem.at[side, 2, g]
            )

        def result(g):
            return pltpu.make_async_copy(os.at[g], o_ref.at[:, :, :, lanes(g)], out_sem)

        def remote(src, dst, send, recv, to):
            return pltpu.make_async_remote_copy(
                src_ref=src,
                dst_ref=dst,
                send_sem=send_sem.at[send],
                recv_sem=recv,
                device_id=to,
                device_id_type=MESH,
            )

        x_from, x_into = (2, 1), (0, 3)
        step_to = ((t + 1, h), (t - 1, h))
        x_sends, x_gets = (has_next, has_prev), (has_prev, has_next)
        detours = ((mid - 1, ends[1], mid), (mid, ends[0], mid - 1))
        turn = height_count // 2
        outer = (h < 2) | (h >= height_count - 2)
        inner_rows = (h >= turn - 2) & (h < turn + 2)
        other = lax.rem(h + turn, height_count)

        def x_copy(way, side, g):
            return remote(
                kv.at[g, side, :, pl.ds(x_from[way], 1)],
                kv.at[g, side, :, pl.ds(x_into[way], 1)],
                way,
                x_sem.at[way, side, g],
                step_to[way],
            )

        def first_leg(way, side, g, row, plane):
            return remote(
                kv.at[g, side, :, pl.ds(x_from[way], 1)],
                hold.at[plane, g],
                way,
                hold_sem.at[plane, g],
                (detours[way][1], row),
            )

        def second_leg(way, side, g, row, plane):
            return remote(
                hold.at[plane, g],
                kv.at[g, side, :, pl.ds(x_into[way], 1)],
                (2, 9, 10, 11)[plane],
                x_sem.at[way, side, g],
                (detours[way][2], row),
            )

        def among(g, chosen):
            found = jnp.bool_(False)
            for one in chosen:
                found = found | (g == one)
            return found

        def goes_round(side, g):
            turns = jnp.logical_not(outer | inner_rows) & among(g, SAME[side])
            turns = turns | (inner_rows & among(g, SAME_INNER[side]))
            return turns | (outer & among(g, SAME_OUTER[side]))

        def goes_far(side, g):
            return among(g, FAR[side])

        def begin_x(side, g):
            for copy in local_kv(side, g):
                copy.wait()
            for way in range(2):
                round_trip = (t == detours[way][0]) & goes_round(side, g)

                @pl.when(round_trip)
                def _():
                    first_leg(way, side, g, h, side).start()

                direct = x_sends[way] & jnp.logical_not(round_trip)
                far_trip = (t == detours[way][0]) & outer & goes_far(side, g)

                @pl.when(far_trip)
                def _():
                    first_leg(way, side, g, other, 2 + side).start()

                direct = direct & jnp.logical_not(far_trip)

                @pl.when(direct)
                def _():
                    x_copy(way, side, g).start()

        def begin_step(step):
            @pl.when(step < heads)
            def _():
                begin_x(0, step)

            @pl.when((step >= heads) & (step < 2 * heads))
            def _():
                begin_x(1, step - heads)

        def arrive_x(way, side, g):
            @pl.when(x_gets[way])
            def _():
                x_copy(way, side, g).wait_recv()

        def pass_on(side, g):
            for way in range(2):

                @pl.when((t == detours[way][1]) & goes_round(side, g))
                def _():
                    first_leg(way, side, g, h, side).wait_recv()
                    second_leg(way, side, g, h, side).start()

                @pl.when((t == detours[way][1]) & inner_rows & goes_far(side, g))
                def _():
                    first_leg(way, side, g, other, 2 + side).wait_recv()
                    second_leg(way, side, g, other, 2 + side).start()

        def q_copy(g):
            return remote(qs.at[g, 0], qn.at[g], 3, q_sem.at[g], (t, far))

        def o_copy(g):
            return remote(send_o.at[g], got_o.at[g], 4, o_sem.at[g], (t, far))

        def l_copy(g):
            return remote(send_l.at[g], got_l.at[g], 5, l_sem.at[g], (t, far))

        def own_copy(g):
            return remote(
                kv.at[g, 1, :, pl.ds(1, frames)],
                sib.at[g, :, pl.ds(1, frames)],
                6,
                own_sem.at[g],
                (t, near),
            )

        def fwd_copy(way, g):
            return remote(
                kv.at[g, 1, :, pl.ds(x_into[way], 1)],
                sib.at[g, :, pl.ds(x_into[way], 1)],
                7 + way,
                fwd_sem.at[way, g],
                (t, near),
            )

        def begin_q(g):
            local_q(0, g).wait()
            q_copy(g).start()

        barrier = pltpu.get_barrier_semaphore()
        greeted = [(has_next, (t + 1, h)), (has_prev, (t - 1, h))]
        greeted += [(is_mid, (at, h)) for at in ends]
        greeted += [(is_end, (at, h)) for at in (mid - 1, mid)]
        greeted += [(is_mid & outer, (at, other)) for at in ends]
        greeted += [(is_end & inner_rows, (at, other)) for at in (mid - 1, mid)]
        total = jnp.int32(1)
        pl.semaphore_signal(barrier, inc=1, device_id=(t, near), device_id_type=MESH)
        for present, place in greeted:
            total = total + present.astype(jnp.int32)

            @pl.when(present)
            def _():
                pl.semaphore_signal(barrier, inc=1, device_id=place, device_id_type=MESH)

        total = total + follows.astype(jnp.int32)

        @pl.when(leads)
        def _():
            pl.semaphore_signal(barrier, inc=1, device_id=(t, far), device_id_type=MESH)

        @pl.loop(0, heads)
        def _(g):
            for copy in local_kv(0, g):
                copy.start()

        sizes = pltpu.make_async_copy(w_hbm, w_ref, w_sem)
        sizes.start()

        @pl.loop(0, heads)
        def _(g):
            local_q(0, g).start()

        pl.semaphore_wait(barrier, total)

        @pl.loop(0, min(X_AHEAD, heads))
        def _(g):
            begin_x(0, g)

        @pl.when(follows)
        def _():
            @pl.loop(0, heads)
            def _(g):
                begin_q(g)

        @pl.loop(0, heads)
        def _(g):
            for copy in local_kv(1, g):
                copy.start()
            local_q(1, g).start()

        @pl.loop(heads, max(X_AHEAD, heads))
        def _(g):
            begin_step(g)

        for present, at in ((has_prev, 0), (has_next, 3)):

            @pl.when(jnp.logical_not(present))
            def _():
                @pl.loop(0, heads)
                def _(g):
                    for part in range(2):
                        for block in (kv.at[g, 0, part, at], kv.at[g, 1, part, at]):
                            block[...] = jnp.zeros(block.shape, block.dtype)
                        sib[g, part, at] = jnp.zeros((half, cols, HD), sib.dtype)

        @pl.when(jnp.logical_not(has_far))
        def _():
            @pl.loop(0, heads)
            def _(g):
                qn[g] = jnp.zeros(qn.shape[1:], qn.dtype)
                got_o[g] = jnp.zeros(got_o.shape[1:], got_o.dtype)
                got_l[g] = jnp.full(got_l.shape[1:], -1e30, got_l.dtype)

        sizes.wait()
        key = lax.broadcasted_iota(jnp.int32, (pair, pair), 1)
        query = lax.broadcasted_iota(jnp.int32, (pair, pair), 0)
        for a in range(2):
            size = []
            for frame in (t * frames - 1 + 2 * a, t * frames + 2 * a):
                inside = (frame >= 0) & (frame < frame_total)
                width = w_ref[jnp.clip(frame, 0, frame_total - 1)]
                size.append(jnp.where(inside, width, 0))
            width = jnp.where(key < quarter, size[0], size[1])
            same = (query < quarter) & (key == query + (1 - a) * quarter)
            ok = (key % cols < width) | same
            bias[a] = jnp.where(ok, 0.0, -1e30).astype(jnp.float32)

        eye = lax.broadcasted_iota(jnp.int32, (quarter, quarter), 0) == (
            lax.broadcasted_iota(jnp.int32, (quarter, quarter), 1)
        )

        def to_row(column):
            return jnp.sum(jnp.where(eye, column, 0.0), axis=0, keepdims=True)

        def to_column(row):
            return jnp.sum(jnp.where(eye, row, 0.0), axis=1, keepdims=True)

        def inner(x, y):
            return lax.dot_general(
                x, y, (((1,), (1,)), ((), ())), preferred_element_type=jnp.float32
            )

        first = lax.broadcasted_iota(jnp.int32, (8, quarter), 0) == 0

        def shares(g):
            logs = []
            for a in range(2):
                q = jnp.concatenate(
                    [qs[g, 0, a].reshape(quarter, HD), qn[g, a].reshape(quarter, HD)], axis=0
                )
                k = kv[g, 0, 0, pl.ds(2 * a, 2)].reshape(pair, HD)
                v = kv[g, 0, 1, pl.ds(2 * a, 2)].reshape(pair, HD)
                s = inner(q, k) + bias[a]
                top = jnp.max(s, axis=1, keepdims=True)
                p = jnp.exp2((s - top) * factor)
                total = jnp.sum(p, axis=1, keepdims=True)
                out = jnp.dot(p.astype(jnp.bfloat16), v, preferred_element_type=jnp.float32)
                out = out * (1.0 / total)
                logs.append(top * factor + jnp.log2(total))
                part_o[g, a] = out[:quarter]
                send_o[g, a] = out[quarter:].astype(jnp.bfloat16).reshape(half, cols, HD)
            part_l[g] = jnp.where(first, to_row(logs[0][:quarter]), to_row(logs[1][:quarter]))
            send_l[g] = jnp.where(first, to_row(logs[0][quarter:]), to_row(logs[1][quarter:]))

        def merge(g):
            @pl.when(has_far)
            def _():
                o_copy(g).wait_recv()
                l_copy(g).wait_recv()

            weight = 1.0 / (1.0 + jnp.exp2(got_l[g] - part_l[g]))
            for a in range(2):
                mine = to_column(weight[a : a + 1])
                other = got_o[g, a].reshape(quarter, HD).astype(jnp.float32)
                out = other + mine * (part_o[g, a] - other)
                os[g, a, pl.ds(first_row[0], half)] = out.astype(jnp.bfloat16).reshape(
                    half, cols, HD
                )

        def whole(g):
            local_q(1, g).wait()
            own_copy(g).wait_recv()
            for way in range(2):

                @pl.when(x_gets[way])
                def _():
                    fwd_copy(way, g).wait_recv()

            for a in range(2):
                q = qs[g, 1, a].reshape(quarter, HD)
                at = pl.ds(2 * a, 2)
                s1 = inner(q, kv[g, 1, 0, at].reshape(pair, HD)) + bias[a, pl.ds(0, quarter)]
                s2 = inner(q, sib[g, 0, at].reshape(pair, HD)) + bias[a, pl.ds(quarter, quarter)]
                top = jnp.maximum(
                    jnp.max(s1, axis=1, keepdims=True), jnp.max(s2, axis=1, keepdims=True)
                )
                p1 = jnp.exp2((s1 - top) * factor)
                p2 = jnp.exp2((s2 - top) * factor)
                total = jnp.sum(p1, axis=1, keepdims=True) + jnp.sum(p2, axis=1, keepdims=True)
                v1 = kv[g, 1, 1, at].reshape(pair, HD)
                v2 = sib[g, 1, at].reshape(pair, HD)
                out = jnp.dot(p1.astype(jnp.bfloat16), v1, preferred_element_type=jnp.float32)
                out += jnp.dot(p2.astype(jnp.bfloat16), v2, preferred_element_type=jnp.float32)
                out = out * (1.0 / total)
                os[g, a, pl.ds(first_row[1], half)] = out.astype(jnp.bfloat16).reshape(
                    half, cols, HD
                )

        @pl.loop(0, PASS_AHEAD)
        def _(g):
            pass_on(0, g)

        def pass_step(step):
            @pl.when(step < heads)
            def _():
                pass_on(0, step)

            @pl.when((step >= heads) & (step < 2 * heads))
            def _():
                pass_on(1, step - heads)

        @pl.loop(0, heads)
        def _(g):
            pass_step(g + PASS_AHEAD)
            arrive_x(0, 0, g)
            arrive_x(1, 0, g)
            begin_step(g + X_AHEAD)

            @pl.when(has_far)
            def _():
                q_copy(g).wait_recv()

            @pl.when(leads & (g == 0))
            def _():
                @pl.loop(0, heads)
                def _(i):
                    begin_q(i)

            @pl.when(jnp.logical_not(has_far))
            def _():
                local_q(0, g).wait()

            shares(g)

            @pl.when(has_far)
            def _():
                o_copy(g).start()
                l_copy(g).start()

        @pl.loop(0, heads + LAG)
        def _(g):
            @pl.when(g >= LAG)
            def _():
                whole(g - LAG)
                result(g - LAG).start()

            @pl.when(g < heads)
            def _():
                own_copy(g).start()
                merge(g)
                pass_step(heads + g + PASS_AHEAD)
                for way in range(2):
                    arrive_x(way, 1, g)

                    @pl.when(x_gets[way])
                    def _():
                        fwd_copy(way, g).start()

                begin_step(heads + g + X_AHEAD)

        def sent(index, ref):
            remote(ref, ref, index, hold_sem.at[0, 0], (t, near)).wait_send()

        for way in range(2):

            @pl.when(x_sends[way])
            def _():
                sent(way, kv.at[:, :, :, pl.ds(x_from[way], 1)])

            @pl.when(x_gets[way])
            def _():
                sent(7 + way, kv.at[:, 1, :, pl.ds(x_into[way], 1)])

        for side, index in ((0, 2), (1, 9)):
            for rows_here, chosen in (
                (jnp.logical_not(outer | inner_rows), SAME[side]),
                (inner_rows, SAME_INNER[side]),
                (outer, SAME_OUTER[side]),
            ):
                if chosen:

                    @pl.when(is_end & rows_here)
                    def _():
                        sent(index, hold.at[side, pl.ds(0, len(chosen))])

            if FAR[side]:

                @pl.when(is_end & inner_rows)
                def _():
                    sent(10 + side, hold.at[2 + side, pl.ds(0, len(FAR[side]))])

        @pl.when(has_far)
        def _():
            sent(3, qn)
            sent(4, send_o)
            sent(5, send_l)

        sent(6, kv.at[:, 1, :, pl.ds(1, frames)])
        pltpu.make_async_copy(os, os, out_sem).wait()

    in_hbm = pl.BlockSpec(memory_space=pl.ANY)
    block = (half, cols, HD)
    return pl.pallas_call(
        kernel,
        out_shape=jax.ShapeDtypeStruct(queries.shape, queries.dtype),
        in_specs=[in_hbm] * 4,
        out_specs=pl.BlockSpec(memory_space=pl.ANY),
        scratch_shapes=[
            pltpu.SMEM(widths.shape, widths.dtype),
            pltpu.VMEM((heads, 2, frames) + block, jnp.bfloat16),
            pltpu.VMEM((heads, frames) + block, jnp.bfloat16),
            pltpu.VMEM((heads, 2, 2, 2 * frames) + block, jnp.bfloat16),
            pltpu.VMEM((heads, 2, 2 * frames) + block, jnp.bfloat16),
            pltpu.VMEM((4, heads, 2, 1) + block, jnp.bfloat16),
            pltpu.VMEM((heads, 2, quarter, HD), jnp.float32),
            pltpu.VMEM((heads, 8, quarter), jnp.float32),
            pltpu.VMEM((heads, frames) + block, jnp.bfloat16),
            pltpu.VMEM((heads, 8, quarter), jnp.float32),
            pltpu.VMEM((heads, frames) + block, jnp.bfloat16),
            pltpu.VMEM((heads, 8, quarter), jnp.float32),
            pltpu.VMEM((heads, frames, rows, cols, HD), jnp.bfloat16),
            pltpu.VMEM((2, pair, pair), jnp.float32),
            pltpu.SemaphoreType.DMA(()),
            pltpu.SemaphoreType.DMA((2, 3, heads)),
            pltpu.SemaphoreType.DMA(()),
            pltpu.SemaphoreType.DMA((12,)),
            pltpu.SemaphoreType.DMA((2, 2, heads)),
            pltpu.SemaphoreType.DMA((heads,)),
            pltpu.SemaphoreType.DMA((heads,)),
            pltpu.SemaphoreType.DMA((heads,)),
            pltpu.SemaphoreType.DMA((heads,)),
            pltpu.SemaphoreType.DMA((2, heads)),
            pltpu.SemaphoreType.DMA((4, heads)),
        ],
        compiler_params=pltpu.CompilerParams(
            collective_id=0, has_side_effects=True, vmem_limit_bytes=VMEM
        ),
    )(widths, queries, keys, values)


def solution(mesh):
    placed = P("tm", "height", None, None)
    return jax.shard_map(
        on_device,
        mesh=mesh,
        in_specs=(placed, placed, placed, P()),
        out_specs=placed,
        check_vma=False,
    )
```
